256 devices in a mesh: row: 16 (over z, core), col: 16 (over x, y).
Axes of the slice: x: 4, y: 4, z: 8, core: 2. Of those that a mesh axis runs over, the one named last changes fastest.
Arguments:
- activations: bfloat16 [2048, 16384], P('row', 'col'), may hold values from -0.26367188 to 0.26367188
- out_grad: bfloat16 [2048, 26624], P('col', 'row'), may hold values from -6 to 6
- weight: bfloat16 [16384, 26624], P('col', 'row'), may hold values from -0.046875 to 0.046875
Outputs:
- input_grad: bfloat16 [2048, 16384], P('row', 'col')
- weight_grad: bfloat16 [16384, 26624], P('col', 'row')
The draws below stay inside these ranges and needn't reach their ends.
All inputs are finite; a program needn't handle non-finite values.
Results may differ from the reference program's by a relative error of at most 0.0012.
Values may be sent and summed in bfloat16 or wider, within the bound.
A program may use at most 128 MiB of HBM per device.

```python
import jax
import jax.numpy as jnp

D = 16384
FF = 26624
TOKENS = 2048


def raised(drawn, key, source, target, blocks, factor):
    owner, partner = [(jnp.arange(drawn.shape[position]) // (drawn.shape[position] // blocks)).reshape([-1 if axis == position else 1 for axis in range(drawn.ndim)]) for position in (source, target)]
    chosen = jax.random.permutation(key, blocks)[partner]
    strong = (owner == chosen) | (owner == (partner + blocks // 2) % blocks)
    return jnp.where(strong, factor * drawn, drawn)


def block_levels(own_key, dims, pieces, low, top_value):
    def one(axis_at, shards_of):
        steps = jax.random.uniform(jax.random.fold_in(jax.random.fold_in(own_key, 6), axis_at), (shards_of,), jnp.float32, low / len(pieces), top_value / len(pieces))
        return jnp.repeat(jnp.exp(steps), dims[axis_at] // shards_of).reshape((-1,) + (1,) * (len(dims) - axis_at - 1))

    level = one(*pieces[0])
    for cut in pieces[1:]:
        level = level * one(*cut)
    return level


def noise(key, shape, spread, bound, pieces=(), kind=jnp.bfloat16):
    entries = spread * jax.random.normal(key, shape, jnp.float32)
    if pieces:
        entries = entries * block_levels(key, shape, pieces, -0.22, 0.18)
    return jnp.clip(entries, -bound, bound).astype(kind)


def gaussian_with(stream_key, extent, width, reach, cuts, heavy, dtype=jnp.bfloat16):
    array = width * jax.random.normal(stream_key, extent, jnp.float32)
    if cuts:
        array = array * block_levels(stream_key, extent, cuts, -0.22, 0.18)
    return jnp.clip(raised(array, jax.random.fold_in(stream_key, 3), *heavy), -reach, reach).astype(dtype)


def setup_inputs(seed: int = 0) -> dict:
    arg_keys = jax.random.split(jax.random.key(seed), 4)
    activations = noise(arg_keys[0], (TOKENS, D), (2.0 / TOKENS ** 0.5), 0.26367188, ((0, 16), (1, 16)))
    out_grad = gaussian_with(arg_keys[1], (TOKENS, FF), 1.0, 6.0, ((0, 16), (1, 16)), (1, 0, 16, 2.0))
    weight = noise(arg_keys[2], (D, FF), D ** -0.5, 0.046875, ((0, 16), (1, 16)))
    return {"activations": activations, "out_grad": out_grad, "weight": weight}


def reference(activations, out_grad, weight):
    input_grad = jnp.dot(out_grad, weight.T, preferred_element_type=jnp.float32).astype(jnp.bfloat16)
    weight_grad = jnp.dot(activations.T, out_grad, preferred_element_type=jnp.float32).astype(jnp.bfloat16)
    return input_grad, weight_grad
```

```python
import functools

import jax
import jax.numpy as jnp
from jax import lax
from jax.experimental import pallas as pl
from jax.experimental.pallas import tpu as pltpu
from jax.sharding import PartitionSpec as P

NX, NY, NZ, NC = 4, 4, 8, 2
TB = 128
HB = TB // 2
QB = TB // 4
DF = 1024
FH = 1664
KC = HB * DF // 128
SCR = 16
REACH = 85.0
MESH = pl.DeviceIdType.MESH
F32, BF16 = jnp.float32, jnp.bfloat16


def rem(a, n):
    return lax.rem(a, n)


def kernel(
    act, og, w, ig_out, wg_out,
    G, AT, ABUF, W, WT, ACC, PT, PR, CS, CR, OUTB,
    ld, gs, gr, zs, zr, sas, sar, pss, psr, css, crs, outs,
):
    row, col = lax.axis_index("row"), lax.axis_index("col")
    z, k = row // NC, rem(row, NC)
    x, y = col // NY, rem(col, NY)

    def dev(dx, dy, dz, flip=False):
        kk = 1 - k if flip else k
        return (rem(z + dz + NZ, NZ) * NC + kk, rem(x + dx + NX, NX) * NY + rem(y + dy + NY, NY))

    def block_row(dx, dy):
        return (rem(x + dx + NX, NX) * NY + rem(y + dy + NY, NY)) * TB

    own = block_row(0, 0)
    load_g = pltpu.make_async_copy(og, G.at[pl.ds(pl.multiple_of(own, TB), TB)], ld.at[0])
    load_a = pltpu.make_async_copy(act, ABUF, ld.at[1])
    load_w = pltpu.make_async_copy(w, W, ld.at[2])
    load_a.start()
    load_g.start()
    load_w.start()

    partners = [dev(1, 0, 0), dev(-1, 0, 0), dev(0, 1, 0), dev(0, -1, 0), dev(0, 0, 1), dev(0, 0, -1), dev(0, 0, 0, True)]
    barrier = pltpu.get_barrier_semaphore()
    for d in partners:
        pl.semaphore_signal(barrier, inc=1, device_id=d, device_id_type=MESH)

    SIGN = (1, -1, 1, -1)

    def g_piece(di, j):
        s = SIGN[di]
        first, second = (0, HB) if di < 2 else (HB, 0)
        sub = 0 if s > 0 else QB
        along, perp, r0, n = (
            (0, 0, first, HB), (0, 0, second, HB), (-s, 0, first + sub, QB),
            (0, -1, second, HB), (0, 1, second, HB), (-s, 0, second + sub, QB),
            (0, 2, second, QB), (0, 2, second + QB, QB),
            (-s, -1, second + sub, QB), (-s, 1, second + sub, QB), (-s, 2, second + sub, QB),
        )[j]
        return along, perp, r0, n

    def g_copy(di, j, shift):
        along, perp, r0, n = g_piece(di, j)
        along = along - shift * SIGN[di]
        dx, dy = (along, perp) if di < 2 else (perp, along)
        ref = G.at[pl.ds(pl.multiple_of(block_row(dx, dy) + r0, QB), n)]
        s = SIGN[di]
        target = dev(s, 0, 0) if di < 2 else dev(0, s, 0)
        return pltpu.make_async_remote_copy(
            src_ref=ref, dst_ref=ref, send_sem=gs.at[di, j], recv_sem=gr.at[di, j],
            device_id=target, device_id_type=MESH)

    def g_send(di, j):
        g_copy(di, j, 0).start()

    def g_round(j):
        for di in range(4):
            s = SIGN[di]
            g_copy(di, j, 1).wait_recv()
            perp = (2, 3) if di < 2 else (0, 1)
            if j == 0:
                g_send(di, 2)
                for p in perp:
                    g_send(p, 3 if s > 0 else 4)
            elif j == 1:
                g_send(di, 5)
            elif j == 2:
                for p in perp:
                    g_send(p, 6 if s > 0 else 7)
            elif j == 3:
                g_send(di, 8)
            elif j == 4:
                g_send(di, 9)
            elif (j == 6 and s > 0) or (j == 7 and s < 0):
                g_send(di, 10)

    def a_ref(n, si, shift):
        s = 1 if si == 0 else -1
        d = (n // 2) if shift == 0 else (n // 2) + 1
        half = n % 2 if si == 0 else 1 - n % 2
        r = rem(z - s * d + NZ, NZ) * NC + k
        return AT.at[r, pl.ds(half * (DF // 2), DF // 2)]

    def a_copy(n, si, shift):
        ref = a_ref(n, si, shift)
        return pltpu.make_async_remote_copy(
            src_ref=ref, dst_ref=ref, send_sem=zs.at[si, n], recv_sem=zr.at[si, n],
            device_id=dev(0, 0, 1 if si == 0 else -1), device_id_type=MESH)

    SIB = (0, 1, -1, 2, -2, 3, -3, 4)

    def sib_copy(i, mine):
        r = rem(z - SIB[i] + NZ, NZ) * NC + (k if mine else 1 - k)
        return pltpu.make_async_remote_copy(
            src_ref=AT.at[r], dst_ref=AT.at[r], send_sem=sas.at[i], recv_sem=sar.at[i],
            device_id=dev(0, 0, 0, True), device_id_type=MESH)

    def a_round(n):
        for si in range(2):
            a_copy(n, si, 1).wait_recv()
            if n <= 4:
                a_copy(n + 2, si, 0).start()
            if n in (1, 3, 5):
                sib_copy(n + si, True).start()
        if n == 6:
            sib_copy(7, True).start()

    def ig_block(dxi, dyi):
        rows = pl.ds(pl.multiple_of(block_row(dxi, dyi), TB), TB)
        idx = dxi * NY + dyi
        for n0 in range(0, DF, 256):
            PT[idx, :, n0:n0 + 256] = jnp.dot(G[rows, :], WT[:, n0:n0 + 256], preferred_element_type=F32)

        @pl.when(rem(dyi + y + k, 2) == 1)
        def _():
            for h in range(2):
                p_copy(dxi, dyi, h).start()

    def p_copy(dxi, dyi, h):
        idx, slot = dxi * NY + dyi, dxi * 2 + dyi // 2
        half = pl.ds(h * HB, HB) if isinstance(h, int) else pl.ds(pl.multiple_of(h * HB, HB), HB)
        return pltpu.make_async_remote_copy(
            src_ref=PT.at[idx, half], dst_ref=PR.at[slot, half], send_sem=pss.at[idx, h], recv_sem=psr.at[slot, h],
            device_id=dev(0, 0, 0, True), device_id_type=MESH)

    def ig_batch(blocks):
        @pl.loop(0, len(blocks))
        def _(i):
            dxi = jnp.int32(blocks[-1][0])
            dyi = jnp.int32(blocks[-1][1])
            for q in range(len(blocks) - 1):
                dxi = jnp.where(i == q, blocks[q][0], dxi)
                dyi = jnp.where(i == q, blocks[q][1], dyi)
            ig_block(dxi, dyi)

    parity = rem(y + k, 2)

    def unit(u):
        m, h = u // 2, rem(u, 2)
        t = jnp.where(parity == 0, rem(m, 4), m // 2)
        dxi = jnp.where(t == 1, 3, jnp.where(t == 2, 1, jnp.where(t == 3, 2, 0)))
        dyi = jnp.where(parity == 0, 2 * (m // 4), 1 + 2 * rem(m, 2))
        bx, by = rem(x + dxi, NX), rem(y + dyi, NY)
        owner = 2 * bx + by // 2
        delta = rem(z - owner + NZ, NZ)
        eps = jnp.where(h == 0, delta, rem(NZ - delta, NZ))
        pos = jnp.where(eps == 0, 4, jnp.where(eps <= 3, 3 - eps, eps - 4))
        return dxi, dyi, h, eps, pos

    def c_copy(u, h, eps):
        step = jnp.where((eps >= 4) == (h == 0), 1, NZ - 1)
        slot = jnp.where(eps == 1, 1, 0)
        return pltpu.make_async_remote_copy(
            src_ref=CS.at[u], dst_ref=CR.at[u, slot], send_sem=css.at[u], recv_sem=crs.at[u, slot],
            device_id=(rem(z + step, NZ) * NC + k, col), device_id_type=MESH)

    def c_wait(u, slot):
        pltpu.make_async_remote_copy(
            src_ref=CS.at[u], dst_ref=CR.at[u, slot], send_sem=css.at[u], recv_sem=crs.at[u, slot],
            device_id=(row, col), device_id_type=MESH).wait_recv()

    def decode(u, slot, r, c, inv):
        code = CR[u, slot, pl.ds(pl.multiple_of(c * HB + r, 16), 16), :].astype(F32)
        mag = (jnp.log(jnp.abs(code)) + REACH) * inv
        return jnp.where(code < 0.0, -mag, mag)

    def reduce_unit(u, p):
        dxi, dyi, h, eps, pos = unit(u)
        idx, slot_p = dxi * NY + dyi, dxi * 2 + dyi // 2

        def total(r, c, invs):
            rr = pl.ds(pl.multiple_of(h * HB + r, 16), 16)
            cc = slice(c * 128, (c + 1) * 128)
            v = PT[idx, rr, cc] + PR[slot_p, rr, cc]
            for slot, inv in enumerate(invs):
                v = v + decode(u, slot, r, c, inv)
            return v

        def scales(n):
            return [CR[u, slot, KC:KC + SCR, :].astype(F32) * (1.0 / (2 * REACH)) for slot in range(n)]

        def relay(n):
            for slot in range(n):
                c_wait(u, slot)
            invs = scales(n)

            def body(i, top):
                r = i * 16
                rr = pl.ds(pl.multiple_of(h * HB + r, 16), 16)
                for c in range(8):
                    v = total(r, c, invs)
                    PT[idx, rr, c * 128:(c + 1) * 128] = v
                    top = jnp.maximum(top, jnp.abs(v))
                return top

            top = lax.fori_loop(0, HB // 16, body, jnp.zeros((16, 128), F32))
            scale = jnp.maximum(top * 1.01, 1e-30).astype(BF16)
            CS[u, KC:KC + SCR, :] = scale
            mul = (2 * REACH) / scale.astype(F32)

            @pl.loop(0, HB // 16)
            def _(i):
                r = i * 16
                rr = pl.ds(pl.multiple_of(h * HB + r, 16), 16)
                for c in range(8):
                    v = PT[idx, rr, c * 128:(c + 1) * 128]
                    code = jnp.exp(jnp.abs(v) * mul - REACH)
                    code = jnp.where(v < 0.0, -code, code)
                    CS[u, pl.ds(pl.multiple_of(c * HB + r, 16), 16), :] = code.astype(BF16)

            c_copy(u, h, eps).start()

        @pl.when(pos == p)
        def _():
            p_copy(dxi, dyi, h).wait_recv()
            if p == 0:
                relay(0)
            elif p < 4:
                relay(1)
            else:
                for slot in range(2):
                    c_wait(u, slot)
                invs = scales(2)

                @pl.loop(0, HB // 16)
                def _(i):
                    r = i * 16
                    rr = pl.ds(pl.multiple_of(h * HB + r, 16), 16)
                    for c in range(8):
                        OUTB[rr, c * 128:(c + 1) * 128] = total(r, c, invs).astype(BF16)

    def reduce_group(m0, m1, p):
        @pl.loop(2 * m0, 2 * m1)
        def _(u):
            reduce_unit(u, p)

    def wg_step(b0, nb, first, last):
        tm = 512
        rows = pl.ds(pl.multiple_of(b0 * TB, TB), nb * TB)

        @pl.loop(0, DF // tm)
        def _(mi):
            mm = pl.ds(pl.multiple_of(mi * tm, tm), tm)
            lhs = jnp.concatenate([AT[b0 + i, mm, :] for i in range(nb)], axis=1)
            for n0 in range(0, FH, 256):
                nn = slice(n0, min(n0 + 256, FH))
                v = jnp.dot(lhs, G[rows, nn], preferred_element_type=F32)
                if last:
                    W[mm, nn] = (ACC[mm, nn] + v).astype(BF16)
                elif first:
                    ACC[mm, nn] = v
                else:
                    ACC[mm, nn] = ACC[mm, nn] + v
            if last:
                pltpu.make_async_copy(W.at[mm], wg_out.at[mm], outs.at[mi]).start()

    def wt_chunk(j):
        WT[j * 128:(j + 1) * 128, :] = W[:, j * 128:(j + 1) * 128].T

    load_a.wait()
    for j in range(DF // 128):
        AT[row, j * 128:(j + 1) * 128, :] = ABUF[:, j * 128:(j + 1) * 128].T
    load_g.wait()
    pl.semaphore_wait(barrier, len(partners))
    for j in range(2):
        for di in range(4):
            g_send(di, j)
        for si in range(2):
            a_copy(j, si, 0).start()
    sib_copy(0, True).start()
    load_w.wait()
    for j in range(6):
        wt_chunk(j)
    a_round(0)
    for j in range(6, 10):
        wt_chunk(j)
    g_round(0)
    a_round(1)
    for j in range(10, FH // 128):
        wt_chunk(j)
    a_round(2)
    g_round(1)
    ig_batch([(0, 0), (1, 0), (3, 0)])
    a_round(3)
    g_round(2)
    ig_batch([(0, 1), (0, 3)])
    a_round(4)
    g_round(3)
    reduce_group(0, 2, 0)
    a_round(5)
    g_round(4)
    a_round(6)
    ig_batch([(3, 3), (3, 1), (1, 3), (1, 1)])
    g_round(5)
    reduce_group(0, 2, 1)
    ig_batch([(2, 0), (0, 2)])
    reduce_group(2, 5, 0)
    g_round(6)
    for i in range(8):
        sib_copy(i, False).wait_recv()
    bown = y // 2
    x1, x2, x3 = rem(x + 1, NX), rem(x + 2, NX), rem(x + 3, NX)
    wg_step(x * NY, 4, True, False)
    g_round(7)
    reduce_group(0, 2, 2)
    g_round(8)
    ig_batch([(3, 2), (2, 3)])
    reduce_group(2, 5, 1)
    reduce_group(0, 2, 3)
    g_round(9)
    ig_batch([(1, 2), (2, 1)])
    reduce_group(5, 7, 0)
    g_round(10)
    ig_batch([(2, 2)])
    reduce_group(7, 8, 0)
    reduce_group(2, 5, 2)
    reduce_group(0, 2, 4)
    wg_step(x1 * NY + 2 * bown, 2, False, False)
    reduce_group(5, 7, 1)
    reduce_group(7, 8, 1)
    reduce_group(2, 5, 3)
    wg_step(x3 * NY + 2 * bown, 2, False, False)
    reduce_group(5, 7, 2)
    reduce_group(7, 8, 2)
    reduce_group(2, 5, 4)
    wg_step(x1 * NY + 2 * (1 - bown), 2, False, False)
    reduce_group(5, 7, 3)
    reduce_group(7, 8, 3)
    wg_step(x3 * NY + 2 * (1 - bown), 2, False, False)
    wg_step(x2 * NY, 4, False, True)
    reduce_group(5, 8, 4)
    out_ig = pltpu.make_async_copy(OUTB, ig_out, ld.at[0])
    out_ig.start()

    for di in range(4):
        for j in range(11):
            g_copy(di, j, 0).wait_send()
    for si in range(2):
        for n in range(7):
            a_copy(n, si, 0).wait_send()
    for i in range(8):
        sib_copy(i, True).wait_send()

    @pl.loop(0, 16)
    def _(i):
        dxi, dyi = i // NY, rem(i, NY)

        @pl.when(rem(dyi + y + k, 2) == 1)
        def _():
            for h in range(2):
                p_copy(dxi, dyi, h).wait_send()

        _, _, h, eps, _ = unit(i)

        @pl.when(eps != 0)
        def _():
            c_copy(i, h, eps).wait_send()

    out_ig.wait()
    for mi in range(2):
        mm = pl.ds(mi * 512, 512)
        pltpu.make_async_copy(W.at[mm], wg_out.at[mm], outs.at[mi]).wait()


def per_device(activations, out_grad, weight):
    dma = pltpu.SemaphoreType.DMA
    vmem = pltpu.VMEM
    nblk = NX * NY
    anywhere = pl.BlockSpec(memory_space=pl.ANY)
    return pl.pallas_call(
        kernel,
        name="up_backward",
        out_shape=(jax.ShapeDtypeStruct((TB, DF), BF16), jax.ShapeDtypeStruct((DF, FH), BF16)),
        in_specs=[anywhere] * 3,
        out_specs=(anywhere, anywhere),
        scratch_shapes=[
            vmem((nblk * TB, FH), BF16),
            vmem((NZ * NC, DF, TB), BF16),
            vmem((TB, DF), BF16),
            vmem((DF, FH), BF16),
            vmem((FH, DF), BF16),
            vmem((DF, FH), F32),
            vmem((nblk, TB, DF), F32),
            vmem((nblk // 2, TB, DF), F32),
            vmem((nblk, KC + SCR, 128), BF16),
            vmem((nblk, 2, KC + SCR, 128), BF16),
            vmem((TB, DF), BF16),
            dma((3,)),
            dma((4, 11)), dma((4, 11)),
            dma((2, 7)), dma((2, 7)),
            dma((8,)), dma((8,)),
            dma((nblk, 2)), dma((nblk // 2, 2)),
            dma((nblk,)), dma((nblk, 2)),
            dma((2,)),
        ],
        cost_estimate=pl.CostEstimate(flops=4 * nblk * TB * DF * FH, bytes_accessed=8 * DF * FH, transcendentals=0),
        compiler_params=pltpu.CompilerParams(
            collective_id=0, has_side_effects=True, vmem_limit_bytes=60 << 20),
    )(activations, out_grad, weight)


def solution(mesh):
    placed = (P("row", "col"), P("col", "row"), P("col", "row"))
    return jax.shard_map(
        per_device,
        mesh=mesh,
        in_specs=placed,
        out_specs=(P("row", "col"), P("col", "row")),
        check_vma=False,
    )
```

```python
import functools

import jax
import jax.numpy as jnp
from jax import lax
from jax.experimental import pallas as pl
from jax.experimental.pallas import tpu as pltpu
from jax.sharding import PartitionSpec as P

NX, NY, NZ, NC = 4, 4, 8, 2
TB = 128
HB = TB // 2
QB = TB // 4
DF = 1024
FH = 1664
DH = DF // 2
KC = TB * DH // 128
SCR = 16
REACH = 85.0
MESH = pl.DeviceIdType.MESH
F32, BF16 = jnp.float32, jnp.bfloat16


TWO = ()
SCHEDULE = (
    ('t', 7), ('t', 6), ('i', ((0, 0),)), ('g', 0), ('a', 0), ('a', 1), ('a', 2), ('g', 1), ('i', ((0, 3), (3, 0))),
    ('a', 3), ('g', 2), ('r', (1,), 0), ('g', 3), ('g', 4), ('a', 4), ('i', ((3, 3), (1, 0), (3, 1))), ('g', 5),
    ('i', ((2, 0), (0, 2))), ('r', (2, 3), 0), ('i', ((0, 1), (1, 3), (1, 1))), ('r', (0,), 0), ('g', 6), ('g', 7),
    ('r', (4,), 0), ('a', 5), ('r', (3,), 1), ('a', 6), ('r', (1,), 1), ('g', 8), ('i', ((3, 2), (2, 3))),
    ('r', (5,), 0), ('g', 9), ('i', ((2, 1),)), ('r', (0, 2), 1), ('i', ((1, 2),)), ('r', (6,), 0), ('g', 10),
    ('i', ((2, 2),)), ('r', (7,), 0), ('s',), ('w', 'x'), ('r', (4, 5, 6), 1), ('r', (0,), 2), ('r', (7,), 1),
    ('w', '3p'), ('r', (1, 2, 3), 2), ('w', '1p'), ('r', (4, 5, 6, 7), 2), ('w', '2'),
    ('r', (0, 1, 2, 3, 4, 5, 6, 7), 3), ('w', '3o'), ('w', '1o'), ('r', (0, 1, 2, 3, 4, 5, 6, 7), 4),
)

def rem(a, n):
    return lax.rem(a, n)


def kernel(
    act, og, w, ig_out, wg_out,
    G, AT, ABUF, W, WT, ACC, PT, PR, CS, CR,
    ld, gs, gr, zs, zr, sas, sar, pss, psr, css, crs,
):
    row, col = lax.axis_index("row"), lax.axis_index("col")
    z, k = row // NC, rem(row, NC)
    x, y = col // NY, rem(col, NY)

    def dev(dx, dy, dz, flip=False):
        kk = 1 - k if flip else k
        return (rem(z + dz + NZ, NZ) * NC + kk, rem(x + dx + NX, NX) * NY + rem(y + dy + NY, NY))

    def block_row(dx, dy):
        return (rem(x + dx + NX, NX) * NY + rem(y + dy + NY, NY)) * TB

    own = block_row(0, 0)
    load_g = pltpu.make_async_copy(og, G.at[pl.ds(pl.multiple_of(own, TB), TB)], ld.at[0])
    load_a = pltpu.make_async_copy(act, ABUF, ld.at[1])
    load_w = pltpu.make_async_copy(w, W, ld.at[2])
    load_a.start()
    load_g.start()
    load_w.start()

    partners = [dev(1, 0, 0), dev(-1, 0, 0), dev(0, 1, 0), dev(0, -1, 0), dev(0, 0, 1), dev(0, 0, -1),
                dev(0, 0, 2), dev(0, 0, -2), dev(0, 0, 0, True)]
    barrier = pltpu.get_barrier_semaphore()
    for d in partners:
        pl.semaphore_signal(barrier, inc=1, device_id=d, device_id_type=MESH)

    SIGN = (1, -1, 1, -1)

    def g_piece(di, j):
        s = SIGN[di]
        first, second = (0, HB) if di < 2 else (HB, 0)
        sub = 0 if s > 0 else QB
        along, perp, r0, n = (
            (0, 0, first, HB), (0, 0, second, HB), (-s, 0, first + sub, QB),
            (0, -1, second, HB), (0, 1, second, HB), (-s, 0, second + sub, QB),
            (0, 2, second, QB), (0, 2, second + QB, QB),
            (-s, -1, second + sub, QB), (-s, 1, second + sub, QB), (-s, 2, second + sub, QB),
        )[j]
        return along, perp, r0, n

    def g_copy(di, j, shift):
        along, perp, r0, n = g_piece(di, j)
        along = along - shift * SIGN[di]
        dx, dy = (along, perp) if di < 2 else (perp, along)
        ref = G.at[pl.ds(pl.multiple_of(block_row(dx, dy) + r0, QB), n)]
        s = SIGN[di]
        target = dev(s, 0, 0) if di < 2 else dev(0, s, 0)
        return pltpu.make_async_remote_copy(
            src_ref=ref, dst_ref=ref, send_sem=gs.at[di, j], recv_sem=gr.at[di, j],
            device_id=target, device_id_type=MESH)

    def g_send(di, j):
        g_copy(di, j, 0).start()

    def g_round(j):
        for di in range(4):
            s = SIGN[di]
            g_copy(di, j, 1).wait_recv()
            perp = (2, 3) if di < 2 else (0, 1)
            if j == 0:
                g_send(di, 2)
                for p in perp:
                    g_send(p, 3 if s > 0 else 4)
            elif j == 1:
                g_send(di, 5)
            elif j == 2:
                for p in perp:
                    g_send(p, 6 if s > 0 else 7)
            elif j == 3:
                g_send(di, 8)
            elif j == 4:
                g_send(di, 9)
            elif (j == 6 and s > 0) or (j == 7 and s < 0):
                g_send(di, 10)

    def a_ref(n, si, shift):
        s = 1 if si == 0 else -1
        d = (n // 2) if shift == 0 else (n // 2) + 1
        half = n % 2 if si == 0 else 1 - n % 2
        r = rem(z - s * d + NZ, NZ) * NC + k
        return AT.at[r, pl.ds(half * (DF // 2), DF // 2)]

    def a_copy(n, si, shift):
        ref = a_ref(n, si, shift)
        return pltpu.make_async_remote_copy(
            src_ref=ref, dst_ref=ref, send_sem=zs.at[si, n], recv_sem=zr.at[si, n],
            device_id=dev(0, 0, 1 if si == 0 else -1), device_id_type=MESH)

    SIB = (0, 1, -1, 2, -2, 3, -3, 4)

    def sib_copy(i, mine):
        r = rem(z - SIB[i] + NZ, NZ) * NC + (k if mine else 1 - k)
        return pltpu.make_async_remote_copy(
            src_ref=AT.at[r], dst_ref=AT.at[r], send_sem=sas.at[i], recv_sem=sar.at[i],
            device_id=dev(0, 0, 0, True), device_id_type=MESH)

    def a_round(n):
        for si in range(2):
            a_copy(n, si, 1).wait_recv()
            if n <= 4:
                a_copy(n + 2, si, 0).start()
            if n in (1, 3, 5):
                sib_copy(n + si, True).start()
        if n == 6:
            sib_copy(7, True).start()

    def pick(i, values):
        v = jnp.int32(values[-1])
        for q, e in enumerate(values[:-1]):
            v = jnp.where(i == q, e, v)
        return v

    def ig_block(dxi, dyi):
        rows = pl.ds(pl.multiple_of(block_row(dxi, dyi), TB), TB)
        idx = dxi * NY + dyi

        @pl.loop(0, 2)
        def _(h):
            for n0 in range(0, DH, 256):
                cols = pl.ds(pl.multiple_of(h * DH + n0, 256), 256)
                PT[idx, h, :, n0:n0 + 256] = jnp.dot(G[rows, :], WT[:, cols], preferred_element_type=F32)

            @pl.when(rem(dyi + y + k, 2) == 1)
            def _():
                p_copy(dxi, dyi, h).start()

    def p_copy(dxi, dyi, h):
        idx, slot = dxi * NY + dyi, dxi * 2 + dyi // 2
        return pltpu.make_async_remote_copy(
            src_ref=PT.at[idx, h], dst_ref=PR.at[slot, h], send_sem=pss.at[idx, h], recv_sem=psr.at[slot, h],
            device_id=dev(0, 0, 0, True), device_id_type=MESH)

    def ig_batch(blocks):
        @pl.loop(0, len(blocks))
        def _(i):
            dxi, dyi = pick(i, [b[0] for b in blocks]), pick(i, [b[1] for b in blocks])
            ig_block(dxi, dyi)

    parity = rem(y + k, 2)

    def unit(u):
        m, h = u // 2, rem(u, 2)
        t = jnp.where(parity == 0, rem(m, 4), m // 2)
        dxi = jnp.where(t == 1, 3, jnp.where(t == 2, 1, jnp.where(t == 3, 2, 0)))
        dyi = jnp.where(parity == 0, 2 * (m // 4), 1 + 2 * rem(m, 2))
        bx, by = rem(x + dxi, NX), rem(y + dyi, NY)
        owner = 2 * bx + by // 2
        delta = rem(z - owner + NZ, NZ)
        eps = jnp.where(h == 0, delta, rem(NZ - delta, NZ))
        return dxi, dyi, h, eps

    def c_copy(u, h, eps, two):
        if two:
            dist = jnp.where((eps == 4) | (eps == 6) | (eps == 2), 2, 1)
            slot = jnp.where((eps == 4) | (eps == 1), 1, jnp.where(eps == 6, 2, jnp.where(eps == 2, 3, 0)))
        else:
            dist = 1
            slot = jnp.where(eps == 1, 1, 0)
        step = jnp.where((eps >= 4) == (h == 0), dist, NZ - dist)
        return pltpu.make_async_remote_copy(
            src_ref=CS.at[u], dst_ref=CR.at[u, slot], send_sem=css.at[u], recv_sem=crs.at[u, slot],
            device_id=(rem(z + step, NZ) * NC + k, col), device_id_type=MESH)

    def c_wait(u, slot):
        pltpu.make_async_remote_copy(
            src_ref=CS.at[u], dst_ref=CR.at[u, slot], send_sem=css.at[u], recv_sem=crs.at[u, slot],
            device_id=(row, col), device_id_type=MESH).wait_recv()

    def decode(u, slot, i, c, inv):
        code = CR[u, slot, pl.ds(pl.multiple_of(c * TB + i * 16, 16), 16), :].astype(F32)
        mag = (jnp.log(jnp.abs(code)) + REACH) * inv
        return jnp.where(code < 0.0, -mag, mag)

    def reduce_unit(u, p, two):
        dxi, dyi, h, eps = unit(u)
        idx, slot_p = dxi * NY + dyi, dxi * 2 + dyi // 2

        def collect(n):
            p_copy(dxi, dyi, h).wait_recv()
            for slot in range(n):
                c_wait(u, slot)
            return [CR[u, slot, KC:KC + SCR, :].astype(F32) * (1.0 / (2 * REACH)) for slot in range(n)]

        def total(i, c, invs):
            rr = pl.ds(pl.multiple_of(i * 16, 16), 16)
            cc = slice(c * 128, (c + 1) * 128)
            v = PT[idx, h, rr, cc] + PR[slot_p, h, rr, cc]
            for slot, inv in enumerate(invs):
                v = v + decode(u, slot, i, c, inv)
            return v

        def relay(n):
            invs = collect(n)

            def body(i, top):
                rr = pl.ds(pl.multiple_of(i * 16, 16), 16)
                for c in range(DH // 128):
                    v = total(i, c, invs)
                    PT[idx, h, rr, c * 128:(c + 1) * 128] = v
                    top = jnp.maximum(top, jnp.abs(v))
                return top

            top = lax.fori_loop(0, TB // 16, body, jnp.zeros((16, 128), F32))
            scale = jnp.maximum(top * 1.01, 1e-30).astype(BF16)
            CS[u, KC:KC + SCR, :] = scale
            mul = (2 * REACH) / scale.astype(F32)

            @pl.loop(0, TB // 16)
            def _(i):
                rr = pl.ds(pl.multiple_of(i * 16, 16), 16)
                for c in range(DH // 128):
                    v = PT[idx, h, rr, c * 128:(c + 1) * 128]
                    code = jnp.exp(jnp.abs(v) * mul - REACH)
                    code = jnp.where(v < 0.0, -code, code)
                    CS[u, pl.ds(pl.multiple_of(c * TB + i * 16, 16), 16), :] = code.astype(BF16)

            c_copy(u, h, eps, two).start()

        def finish(n):
            invs = collect(n)
            for half in range(2):
                @pl.when(h == half)
                def _():
                    @pl.loop(0, TB // 16)
                    def _(i):
                        rr = pl.ds(pl.multiple_of(i * 16, 16), 16)
                        for c in range(DH // 128):
                            c0 = half * DH + c * 128
                            ig_out[rr, c0:c0 + 128] = total(i, c, invs).astype(BF16)

        if two:
            if p == 0:
                pl.when((eps == 1) | (eps == 7) | ((eps >= 3) & (eps <= 5)))(lambda: relay(0))
            elif p == 1:
                pl.when(eps == 6)(lambda: relay(2))
                pl.when(eps == 2)(lambda: relay(1))
            else:
                pl.when(eps == 0)(lambda: finish(4))
        else:
            if p == 0:
                pl.when((eps == 4) | (eps == 3))(lambda: relay(0))
            elif p < 4:
                pl.when((eps == 4 + p) | ((eps == 3 - p) & (eps > 0)))(lambda: relay(1))
            else:
                pl.when(eps == 0)(lambda: finish(2))

    def reduce_group(ms, p):
        @pl.loop(0, 2 * len(ms))
        def _(i):
            reduce_unit(2 * pick(i // 2, ms) + rem(i, 2), p, ms[0] in TWO)

    def wg_step(b0, nb, first, last):
        tm = 512
        rows = pl.ds(pl.multiple_of(b0 * TB, TB), nb * TB)

        @pl.loop(0, DF // tm)
        def _(mi):
            mm = pl.ds(pl.multiple_of(mi * tm, tm), tm)
            lhs = jnp.concatenate([AT[b0 + i, mm, :] for i in range(nb)], axis=1)
            for n0 in range(0, FH, 256):
                nn = slice(n0, min(n0 + 256, FH))
                v = jnp.dot(lhs, G[rows, nn], preferred_element_type=F32)
                if last:
                    wg_out[mm, nn] = (ACC[mm, nn] + v).astype(BF16)
                elif first:
                    ACC[mm, nn] = v
                else:
                    ACC[mm, nn] = ACC[mm, nn] + v

    def wt_chunk(j):
        WT[j * 128:(j + 1) * 128, :] = W[:, j * 128:(j + 1) * 128].T

    load_a.wait()
    for j in range(DF // 128):
        AT[row, j * 128:(j + 1) * 128, :] = ABUF[:, j * 128:(j + 1) * 128].T
    load_g.wait()
    pl.semaphore_wait(barrier, len(partners))
    for j in range(2):
        for di in range(4):
            g_send(di, j)
        for si in range(2):
            a_copy(j, si, 0).start()
    sib_copy(0, True).start()
    load_w.wait()
    bown = y // 2
    x1, x2, x3 = rem(x + 1, NX), rem(x + 2, NX), rem(x + 3, NX)
    groups = {
        "x": (x * NY, 4), "2": (x2 * NY, 4),
        "1o": (x1 * NY + 2 * bown, 2), "1p": (x1 * NY + 2 * (1 - bown), 2),
        "3o": (x3 * NY + 2 * bown, 2), "3p": (x3 * NY + 2 * (1 - bown), 2),
    }
    wt_next, wg_done = 0, 0
    for what, *how in SCHEDULE:
        if what == "t":
            for j in range(wt_next, wt_next + how[0]):
                wt_chunk(j)
            wt_next += how[0]
        elif what == "g":
            g_round(how[0])
        elif what == "a":
            a_round(how[0])
        elif what == "i":
            ig_batch(how[0])
        elif what == "s":
            for i in range(8):
                sib_copy(i, False).wait_recv()
        elif what == "w":
            wg_step(*groups[how[0]], wg_done == 0, wg_done == 5)
            wg_done += 1
        else:
            reduce_group(*how)

    for di in range(4):
        for j in range(11):
            g_copy(di, j, 0).wait_send()
    for si in range(2):
        for n in range(7):
            a_copy(n, si, 0).wait_send()
    for i in range(8):
        sib_copy(i, True).wait_send()

    @pl.loop(0, 16)
    def _(i):
        dxi, dyi = i // NY, rem(i, NY)

        @pl.when(rem(dyi + y + k, 2) == 1)
        def _():
            for h in range(2):
                p_copy(dxi, dyi, h).wait_send()

        _, _, h, eps = unit(i)

        @pl.when(eps != 0)
        def _():
            c_copy(i, h, eps, False).wait_send()


def hand_out(ig, wg, ig_out, wg_out, sems):
    n = sems.shape[0] - 1
    rows = DF // n
    copies = [pltpu.make_async_copy(wg.at[pl.ds(i * rows, rows)], wg_out.at[pl.ds(i * rows, rows)], sems.at[i])
              for i in range(n)]
    copies.append(pltpu.make_async_copy(ig, ig_out, sems.at[n]))
    for c in copies:
        c.start()
    for c in copies:
        c.wait()


def per_device(activations, out_grad, weight):
    dma = pltpu.SemaphoreType.DMA
    vmem = pltpu.VMEM
    nblk = NX * NY
    anywhere = pl.BlockSpec(memory_space=pl.ANY)
    sums = pl.pallas_call(
        kernel,
        name="up_backward",
        out_shape=(vmem((TB, DF), BF16), vmem((DF, FH), BF16)),
        in_specs=[anywhere] * 3,
        out_specs=(pl.BlockSpec(memory_space=vmem),) * 2,
        scratch_shapes=[
            vmem((nblk * TB, FH), BF16),
            vmem((NZ * NC, DF, TB), BF16),
            vmem((TB, DF), BF16),
            vmem((DF, FH), BF16),
            vmem((FH, DF), BF16),
            vmem((DF, FH), F32),
            vmem((nblk, 2, TB, DH), F32),
            vmem((nblk // 2, 2, TB, DH), F32),
            vmem((nblk, KC + SCR, 128), BF16),
            vmem((nblk, 4, KC + SCR, 128), BF16),
            dma((3,)),
            dma((4, 11)), dma((4, 11)),
            dma((2, 7)), dma((2, 7)),
            dma((8,)), dma((8,)),
            dma((nblk, 2)), dma((nblk // 2, 2)),
            dma((nblk,)), dma((nblk, 4)),
        ],
        cost_estimate=pl.CostEstimate(flops=4 * nblk * TB * DF * FH, bytes_accessed=8 * DF * FH, transcendentals=0),
        compiler_params=pltpu.CompilerParams(
            collective_id=0, has_side_effects=True, vmem_limit_bytes=52 << 20),
    )(activations, out_grad, weight)
    return pl.pallas_call(
        hand_out,
        name="hand_out",
        out_shape=(jax.ShapeDtypeStruct((TB, DF), BF16), jax.ShapeDtypeStruct((DF, FH), BF16)),
        in_specs=[pl.BlockSpec(memory_space=vmem)] * 2,
        out_specs=(anywhere, anywhere),
        scratch_shapes=[dma((17,))],
    )(*sums)


def solution(mesh):
    placed = (P("row", "col"), P("col", "row"), P("col", "row"))
    return jax.shard_map(
        per_device,
        mesh=mesh,
        in_specs=placed,
        out_specs=(P("row", "col"), P("col", "row")),
        check_vma=False,
    )
```

```python
import functools

import jax
import jax.numpy as jnp
from jax import lax
from jax.experimental import pallas as pl
from jax.experimental.pallas import tpu as pltpu
from jax.sharding import PartitionSpec as P

NX, NY, NZ, NC = 4, 4, 8, 2
TB = 128
HB = TB // 2
QB = TB // 4
DF = 1024
FH = 1664
DH = DF // 2
KC = TB * DH // 128
SCR = 16
REACH = 85.0
MESH = pl.DeviceIdType.MESH
F32, BF16 = jnp.float32, jnp.bfloat16


TWO = ()
SCHEDULE = (
    ('t', 7), ('t', 6), ('i', ((0, 0),)), ('a', 0), ('g', 0), ('g', 1), ('i', ((0, 1), (0, 3))), ('a', 1),
    ('i', ((1, 0), (3, 0))), ('a', 2), ('a', 3), ('g', 2), ('r', (0,), 0), ('g', 3), ('g', 4),
    ('i', ((3, 3), (3, 1))), ('a', 4), ('i', ((1, 3), (1, 1))), ('g', 5), ('r', (2,), 0), ('i', ((2, 0), (0, 2))),
    ('r', (3, 4), 0), ('g', 6), ('g', 7), ('r', (1,), 0), ('r', (3,), 1), ('a', 5), ('g', 8), ('i', ((3, 2), (2, 3))),
    ('r', (5,), 0), ('a', 6), ('r', (2,), 1), ('g', 9), ('i', ((1, 2), (2, 1))), ('r', (3,), 2), ('r', (4,), 1),
    ('r', (6,), 0), ('r', (0,), 1), ('s',), ('g', 10), ('i', ((2, 2),)), ('r', (7,), 0), ('w', '1', 1),
    ('r', (5,), 1), ('w', '0', 1), ('r', (1, 6), 1), ('w', '2', 0), ('r', (2,), 2), ('r', (7,), 1), ('r', (0,), 2),
    ('w', '0', 0), ('r', (1, 4, 5), 2), ('w', '3', 0), ('r', (6,), 2), ('w', '3', 1), ('r', (7,), 2),
    ('r', (0, 1, 4, 5), 3), ('w', '1', 0), ('r', (2, 3), 3), ('w', '2', 1), ('r', (7,), 3), ('r', (4,), 4),
    ('r', (6,), 3), ('r', (0, 1, 2, 3, 5, 6, 7), 4),
)

def rem(a, n):
    return lax.rem(a, n)


def kernel(
    act, og, w, ig_out, wg_out,
    G, AT, ABUF, W, WT, ACC, PT, PR, CS, CR,
    ld, gs, gr, zs, zr, sas, sar, pss, psr, css, crs,
):
    row, col = lax.axis_index("row"), lax.axis_index("col")
    z, k = row // NC, rem(row, NC)
    x, y = col // NY, rem(col, NY)

    def dev(dx, dy, dz, flip=False):
        kk = 1 - k if flip else k
        return (rem(z + dz + NZ, NZ) * NC + kk, rem(x + dx + NX, NX) * NY + rem(y + dy + NY, NY))

    def block_row(dx, dy):
        return (rem(x + dx + NX, NX) * NY + rem(y + dy + NY, NY)) * TB

    own = block_row(0, 0)
    load_g = pltpu.make_async_copy(og, G.at[pl.ds(pl.multiple_of(own, TB), TB)], ld.at[0])
    load_a = pltpu.make_async_copy(act, ABUF, ld.at[1])
    load_w = pltpu.make_async_copy(w, W, ld.at[2])
    load_a.start()
    load_g.start()
    load_w.start()

    partners = [dev(1, 0, 0), dev(-1, 0, 0), dev(0, 1, 0), dev(0, -1, 0), dev(0, 0, 1), dev(0, 0, -1),
                dev(0, 0, 2), dev(0, 0, -2), dev(0, 0, 0, True)]
    barrier = pltpu.get_barrier_semaphore()
    for d in partners:
        pl.semaphore_signal(barrier, inc=1, device_id=d, device_id_type=MESH)

    SIGN = (1, -1, 1, -1)

    def g_piece(di, j):
        s = SIGN[di]
        first, second = (0, HB) if di < 2 else (HB, 0)
        sub = 0 if s > 0 else QB
        along, perp, r0, n = (
            (0, 0, first, HB), (0, 0, second, HB), (-s, 0, first + sub, QB),
            (0, -1, second, HB), (0, 1, second, HB), (-s, 0, second + sub, QB),
            (0, 2, second, QB), (0, 2, second + QB, QB),
            (-s, -1, second + sub, QB), (-s, 1, second + sub, QB), (-s, 2, second + sub, QB),
        )[j]
        return along, perp, r0, n

    def g_copy(di, j, shift):
        along, perp, r0, n = g_piece(di, j)
        along = along - shift * SIGN[di]
        dx, dy = (along, perp) if di < 2 else (perp, along)
        ref = G.at[pl.ds(pl.multiple_of(block_row(dx, dy) + r0, QB), n)]
        s = SIGN[di]
        target = dev(s, 0, 0) if di < 2 else dev(0, s, 0)
        return pltpu.make_async_remote_copy(
            src_ref=ref, dst_ref=ref, send_sem=gs.at[di, j], recv_sem=gr.at[di, j],
            device_id=target, device_id_type=MESH)

    def g_send(di, j):
        g_copy(di, j, 0).start()

    def g_round(j):
        for di in range(4):
            s = SIGN[di]
            g_copy(di, j, 1).wait_recv()
            perp = (2, 3) if di < 2 else (0, 1)
            if j == 0:
                g_send(di, 2)
                for p in perp:
                    g_send(p, 3 if s > 0 else 4)
            elif j == 1:
                g_send(di, 5)
            elif j == 2:
                for p in perp:
                    g_send(p, 6 if s > 0 else 7)
            elif j == 3:
                g_send(di, 8)
            elif j == 4:
                g_send(di, 9)
            elif (j == 6 and s > 0) or (j == 7 and s < 0):
                g_send(di, 10)

    def a_ref(n, si, shift):
        s = 1 if si == 0 else -1
        d = (n // 2) if shift == 0 else (n // 2) + 1
        half = n % 2 if si == 0 else 1 - n % 2
        r = rem(z - s * d + NZ, NZ) * NC + k
        return AT.at[r, pl.ds(half * (DF // 2), DF // 2)]

    def a_copy(n, si, shift):
        ref = a_ref(n, si, shift)
        return pltpu.make_async_remote_copy(
            src_ref=ref, dst_ref=ref, send_sem=zs.at[si, n], recv_sem=zr.at[si, n],
            device_id=dev(0, 0, 1 if si == 0 else -1), device_id_type=MESH)

    SIB = (0, 1, -1, 2, -2, 3, -3, 4)

    def sib_copy(i, mine):
        r = rem(z - SIB[i] + NZ, NZ) * NC + (k if mine else 1 - k)
        return pltpu.make_async_remote_copy(
            src_ref=AT.at[r], dst_ref=AT.at[r], send_sem=sas.at[i], recv_sem=sar.at[i],
            device_id=dev(0, 0, 0, True), device_id_type=MESH)

    def a_round(n):
        for si in range(2):
            a_copy(n, si, 1).wait_recv()
            if n <= 4:
                a_copy(n + 2, si, 0).start()
            if n in (1, 3, 5):
                sib_copy(n + si, True).start()
        if n == 6:
            sib_copy(7, True).start()

    def pick(i, values):
        v = jnp.int32(values[-1])
        for q, e in enumerate(values[:-1]):
            v = jnp.where(i == q, e, v)
        return v

    def ig_blocks(blocks):
        rows = [pl.ds(pl.multiple_of(block_row(dxi, dyi), TB), TB) for dxi, dyi in blocks]

        for h in range(2):
            for n0 in range(0, DH, 256):
                lhs = jnp.concatenate([G[r, :] for r in rows], axis=0)
                d = jnp.dot(lhs, WT[:, h * DH + n0:h * DH + n0 + 256], preferred_element_type=F32)
                for i, (dxi, dyi) in enumerate(blocks):
                    PT[dxi * NY + dyi, h, :, n0:n0 + 256] = d[i * TB:(i + 1) * TB]
            for dxi, dyi in blocks:
                @pl.when(rem(dyi + y + k, 2) == 1)
                def _():
                    p_copy(dxi, dyi, h).start()

    def p_copy(dxi, dyi, h):
        idx, slot = dxi * NY + dyi, dxi * 2 + dyi // 2
        return pltpu.make_async_remote_copy(
            src_ref=PT.at[idx, h], dst_ref=PR.at[slot, h], send_sem=pss.at[idx, h], recv_sem=psr.at[slot, h],
            device_id=dev(0, 0, 0, True), device_id_type=MESH)

    parity = rem(y + k, 2)

    def unit(u):
        m, h = u // 2, rem(u, 2)
        t = jnp.where(parity == 0, rem(m, 4), m // 2)
        dxi = jnp.where(t == 1, 3, jnp.where(t == 2, 1, jnp.where(t == 3, 2, 0)))
        dyi = jnp.where(parity == 0, 2 * (m // 4), 1 + 2 * rem(m, 2))
        bx, by = rem(x + dxi, NX), rem(y + dyi, NY)
        owner = 2 * bx + by // 2
        delta = rem(z - owner + NZ, NZ)
        eps = jnp.where(h == 0, delta, rem(NZ - delta, NZ))
        return dxi, dyi, h, eps

    def c_copy(u, h, eps, two):
        if two:
            dist = jnp.where((eps == 4) | (eps == 6) | (eps == 2), 2, 1)
            slot = jnp.where((eps == 4) | (eps == 1), 1, jnp.where(eps == 6, 2, jnp.where(eps == 2, 3, 0)))
        else:
            dist = 1
            slot = jnp.where(eps == 1, 1, 0)
        step = jnp.where((eps >= 4) == (h == 0), dist, NZ - dist)
        return pltpu.make_async_remote_copy(
            src_ref=CS.at[u], dst_ref=CR.at[u, slot], send_sem=css.at[u], recv_sem=crs.at[u, slot],
            device_id=(rem(z + step, NZ) * NC + k, col), device_id_type=MESH)

    def c_wait(u, slot):
        pltpu.make_async_remote_copy(
            src_ref=CS.at[u], dst_ref=CR.at[u, slot], send_sem=css.at[u], recv_sem=crs.at[u, slot],
            device_id=(row, col), device_id_type=MESH).wait_recv()

    def decode(u, slot, i, c, inv):
        code = CR[u, slot, pl.ds(pl.multiple_of(c * TB + i * 16, 16), 16), :].astype(F32)
        mag = (jnp.log(jnp.abs(code)) + REACH) * inv
        return jnp.where(code < 0.0, -mag, mag)

    def reduce_unit(u, p, two):
        dxi, dyi, h, eps = unit(u)
        idx, slot_p = dxi * NY + dyi, dxi * 2 + dyi // 2

        def collect(n):
            p_copy(dxi, dyi, h).wait_recv()
            for slot in range(n):
                c_wait(u, slot)
            return [CR[u, slot, KC:KC + SCR, :].astype(F32) * (1.0 / (2 * REACH)) for slot in range(n)]

        def total(i, c, invs):
            rr = pl.ds(pl.multiple_of(i * 16, 16), 16)
            cc = slice(c * 128, (c + 1) * 128)
            v = PT[idx, h, rr, cc] + PR[slot_p, h, rr, cc]
            for slot, inv in enumerate(invs):
                v = v + decode(u, slot, i, c, inv)
            return v

        def relay(n):
            invs = collect(n)

            def body(i, top):
                rr = pl.ds(pl.multiple_of(i * 16, 16), 16)
                for c in range(DH // 128):
                    v = total(i, c, invs)
                    PT[idx, h, rr, c * 128:(c + 1) * 128] = v
                    top = jnp.maximum(top, jnp.abs(v))
                return top

            top = lax.fori_loop(0, TB // 16, body, jnp.zeros((16, 128), F32), unroll=TB // 16)
            scale = jnp.maximum(top * 1.01, 1e-30).astype(BF16)
            CS[u, KC:KC + SCR, :] = scale
            mul = (2 * REACH) / scale.astype(F32)

            @pl.loop(0, TB // 16, unroll=TB // 16)
            def _(i):
                rr = pl.ds(pl.multiple_of(i * 16, 16), 16)
                for c in range(DH // 128):
                    v = PT[idx, h, rr, c * 128:(c + 1) * 128]
                    code = jnp.exp(jnp.abs(v) * mul - REACH)
                    code = jnp.where(v < 0.0, -code, code)
                    CS[u, pl.ds(pl.multiple_of(c * TB + i * 16, 16), 16), :] = code.astype(BF16)

            c_copy(u, h, eps, two).start()

        def finish(n):
            invs = collect(n)
            for half in range(2):
                @pl.when(h == half)
                def _():
                    @pl.loop(0, TB // 16, unroll=TB // 16)
                    def _(i):
                        rr = pl.ds(pl.multiple_of(i * 16, 16), 16)
                        for c in range(DH // 128):
                            c0 = half * DH + c * 128
                            ig_out[rr, c0:c0 + 128] = total(i, c, invs).astype(BF16)

        if two:
            if p == 0:
                pl.when((eps == 1) | (eps == 7) | ((eps >= 3) & (eps <= 5)))(lambda: relay(0))
            elif p == 1:
                pl.when(eps == 6)(lambda: relay(2))
                pl.when(eps == 2)(lambda: relay(1))
            else:
                pl.when(eps == 0)(lambda: finish(4))
        else:
            if p == 0:
                pl.when((eps == 4) | (eps == 3))(lambda: relay(0))
            elif p < 4:
                pl.when((eps == 4 + p) | ((eps == 3 - p) & (eps > 0)))(lambda: relay(1))
            else:
                pl.when(eps == 0)(lambda: finish(2))

    def reduce_group(ms, p):
        @pl.loop(0, 2 * len(ms))
        def _(i):
            reduce_unit(2 * pick(i // 2, ms) + rem(i, 2), p, ms[0] in TWO)

    def wg_step(b0, n0, n1, first, last):
        rows = pl.ds(pl.multiple_of(b0 * TB, TB), NY * TB)
        lhs = jnp.concatenate([AT[b0 + i] for i in range(NY)], axis=1)
        for n in range(n0, n1, 256):
            nn = slice(n, min(n + 256, n1))
            v = jnp.dot(lhs, G[rows, nn], preferred_element_type=F32)
            if last:
                wg_out[:, nn] = (ACC[:, nn] + v).astype(BF16)
            elif first:
                ACC[:, nn] = v
            else:
                ACC[:, nn] = ACC[:, nn] + v

    def wt_chunk(j):
        WT[j * 128:(j + 1) * 128, :] = W[:, j * 128:(j + 1) * 128].T

    load_a.wait()
    for j in range(DF // 128):
        AT[row, j * 128:(j + 1) * 128, :] = ABUF[:, j * 128:(j + 1) * 128].T
    load_g.wait()
    pl.semaphore_wait(barrier, len(partners))
    for j in range(2):
        for di in range(4):
            g_send(di, j)
        for si in range(2):
            a_copy(j, si, 0).start()
    sib_copy(0, True).start()
    load_w.wait()
    groups = {name: rem(x + int(name), NX) * NY for name in "0123"}
    wt_next, wg_done = 0, [0, 0]
    columns = ((0, 1024), (1024, FH))
    for what, *how in SCHEDULE:
        if what == "t":
            for j in range(wt_next, wt_next + how[0]):
                wt_chunk(j)
            wt_next += how[0]
        elif what == "g":
            g_round(how[0])
        elif what == "a":
            a_round(how[0])
        elif what == "i":
            ig_blocks(how[0])
        elif what == "s":
            for i in range(8):
                sib_copy(i, False).wait_recv()
        elif what == "w":
            part = how[1]
            wg_step(groups[how[0]], *columns[part], wg_done[part] == 0, wg_done[part] == 3)
            wg_done[part] += 1
        else:
            reduce_group(*how)

    for di in range(4):
        for j in range(11):
            g_copy(di, j, 0).wait_send()
    for si in range(2):
        for n in range(7):
            a_copy(n, si, 0).wait_send()
    for i in range(8):
        sib_copy(i, True).wait_send()

    @pl.loop(0, 16)
    def _(i):
        dxi, dyi = i // NY, rem(i, NY)

        @pl.when(rem(dyi + y + k, 2) == 1)
        def _():
            for h in range(2):
                p_copy(dxi, dyi, h).wait_send()

        _, _, h, eps = unit(i)

        @pl.when(eps != 0)
        def _():
            c_copy(i, h, eps, False).wait_send()


def hand_out(ig, wg, ig_out, wg_out, sems):
    n = sems.shape[0] - 1
    rows = DF // n
    copies = [pltpu.make_async_copy(wg.at[pl.ds(i * rows, rows)], wg_out.at[pl.ds(i * rows, rows)], sems.at[i])
              for i in range(n)]
    copies.append(pltpu.make_async_copy(ig, ig_out, sems.at[n]))
    for c in copies:
        c.start()
    for c in copies:
        c.wait()


def per_device(activations, out_grad, weight):
    dma = pltpu.SemaphoreType.DMA
    vmem = pltpu.VMEM
    nblk = NX * NY
    anywhere = pl.BlockSpec(memory_space=pl.ANY)
    sums = pl.pallas_call(
        kernel,
        name="up_backward",
        out_shape=(vmem((TB, DF), BF16), vmem((DF, FH), BF16)),
        in_specs=[anywhere] * 3,
        out_specs=(pl.BlockSpec(memory_space=vmem),) * 2,
        scratch_shapes=[
            vmem((nblk * TB, FH), BF16),
            vmem((NZ * NC, DF, TB), BF16),
            vmem((TB, DF), BF16),
            vmem((DF, FH), BF16),
            vmem((FH, DF), BF16),
            vmem((DF, FH), F32),
            vmem((nblk, 2, TB, DH), F32),
            vmem((nblk // 2, 2, TB, DH), F32),
            vmem((nblk, KC + SCR, 128), BF16),
            vmem((nblk, 4, KC + SCR, 128), BF16),
            dma((3,)),
            dma((4, 11)), dma((4, 11)),
            dma((2, 7)), dma((2, 7)),
            dma((8,)), dma((8,)),
            dma((nblk, 2)), dma((nblk // 2, 2)),
            dma((nblk,)), dma((nblk, 4)),
        ],
        cost_estimate=pl.CostEstimate(flops=4 * nblk * TB * DF * FH, bytes_accessed=8 * DF * FH, transcendentals=0),
        compiler_params=pltpu.CompilerParams(
            collective_id=0, has_side_effects=True, vmem_limit_bytes=52 << 20),
    )(activations, out_grad, weight)
    return pl.pallas_call(
        hand_out,
        name="hand_out",
        out_shape=(jax.ShapeDtypeStruct((TB, DF), BF16), jax.ShapeDtypeStruct((DF, FH), BF16)),
        in_specs=[pl.BlockSpec(memory_space=vmem)] * 2,
        out_specs=(anywhere, anywhere),
        scratch_shapes=[dma((17,))],
        compiler_params=pltpu.CompilerParams(vmem_limit_bytes=1 << 20),
    )(*sums)


def solution(mesh):
    placed = (P("row", "col"), P("col", "row"), P("col", "row"))
    return jax.shard_map(
        per_device,
        mesh=mesh,
        in_specs=placed,
        out_specs=(P("row", "col"), P("col", "row")),
        check_vma=False,
    )
```

```python
import functools

import jax
import jax.numpy as jnp
from jax import lax
from jax.experimental import pallas as pl
from jax.experimental.pallas import tpu as pltpu
from jax.sharding import PartitionSpec as P

NX, NY, NZ, NC = 4, 4, 8, 2
TB = 128
HB = TB // 2
QB = TB // 4
DF = 1024
FH = 1664
DH = DF // 2
KC = TB * DH // 128
SCR = 16
REACH = 85.0
MESH = pl.DeviceIdType.MESH
F32, BF16 = jnp.float32, jnp.bfloat16


SCHEDULE = (
    ('t', 7), ('t', 6), ('g', 0), ('a', 0), ('a', 1), ('a', 2), ('g', 1), ('i', ((0, 1), (0, 3))), ('g', 2), ('a', 3),
    ('i', ((1, 0), (3, 0))), ('r', 'first', (1,)), ('i', ((0, 0),)), ('g', 3), ('g', 4), ('r', 'first', (0,)),
    ('i', ((3, 3), (3, 1))), ('a', 4), ('i', ((1, 3), (1, 1))), ('r', 'middle', ((1, 1),)), ('g', 5),
    ('i', ((2, 0), (0, 2))), ('r', 'first', (3,)), ('g', 6), ('r', 'first', (2,)), ('g', 7), ('r', 'first', (4,)),
    ('a', 5), ('a', 6), ('g', 8), ('i', ((3, 2), (2, 3))), ('r', 'middle', ((3, 1), (1, 2))), ('r', 'first', (5,)),
    ('r', 'middle', ((2, 1),)), ('g', 9), ('i', ((1, 2), (2, 1))), ('g', 10), ('r', 'first', (6,)), ('i', ((2, 2),)),
    ('r', 'first', (7,)), ('r', 'middle', ((0, 1),)), ('s',), ('w', '1', 0), ('r', 'middle', ((4, 1), (5, 1))),
    ('w', '2', 1), ('r', 'middle', ((2, 2), (6, 1), (7, 1))), ('w', '0', 0), ('r', 'middle', ((3, 2), (0, 2))),
    ('w', '1', 1), ('r', 'middle', ((5, 2), (4, 2))), ('w', '2', 0), ('r', 'middle', ((6, 2), (7, 2))), ('w', '3', 1),
    ('w', '3', 0), ('r', 'middle', ((4, 3), (0, 3), (2, 3), (5, 3), (3, 3), (6, 3), (7, 3), (1, 3))), ('w', '0', 1),
    ('r', 'last', (2, 1, 5, 3, 4, 0, 6, 7)),
)

def rem(a, n):
    return lax.rem(a, n)


def kernel(
    act, og, w, ig_out, wg_out,
    G, AT, ABUF, W, WT, ACC, PT, PR, CS, CR,
    ld, gs, gr, zs, zr, sas, sar, pss, psr, css, crs,
):
    row, col = lax.axis_index("row"), lax.axis_index("col")
    z, k = row // NC, rem(row, NC)
    x, y = col // NY, rem(col, NY)

    def dev(dx, dy, dz, flip=False):
        kk = 1 - k if flip else k
        return (rem(z + dz + NZ, NZ) * NC + kk, rem(x + dx + NX, NX) * NY + rem(y + dy + NY, NY))

    def block_row(dx, dy):
        return (rem(x + dx + NX, NX) * NY + rem(y + dy + NY, NY)) * TB

    own = block_row(0, 0)
    load_g = pltpu.make_async_copy(og, G.at[pl.ds(pl.multiple_of(own, TB), TB)], ld.at[0])
    load_a = pltpu.make_async_copy(act, ABUF, ld.at[1])
    load_w = pltpu.make_async_copy(w, W, ld.at[2])
    load_a.start()
    load_g.start()
    load_w.start()

    partners = [dev(1, 0, 0), dev(-1, 0, 0), dev(0, 1, 0), dev(0, -1, 0), dev(0, 0, 1), dev(0, 0, -1),
                dev(0, 0, 0, True)]
    barrier = pltpu.get_barrier_semaphore()
    for d in partners:
        pl.semaphore_signal(barrier, inc=1, device_id=d, device_id_type=MESH)

    SIGN = (1, -1, 1, -1)

    def g_piece(di, j):
        s = SIGN[di]
        first, second = (0, HB) if di < 2 else (HB, 0)
        sub = 0 if s > 0 else QB
        along, perp, r0, n = (
            (0, 0, first, HB), (0, 0, second, HB), (-s, 0, first + sub, QB),
            (0, -1, second, HB), (0, 1, second, HB), (-s, 0, second + sub, QB),
            (0, 2, second, QB), (0, 2, second + QB, QB),
            (-s, -1, second + sub, QB), (-s, 1, second + sub, QB), (-s, 2, second + sub, QB),
        )[j]
        return along, perp, r0, n

    def g_copy(di, j, shift):
        along, perp, r0, n = g_piece(di, j)
        along = along - shift * SIGN[di]
        dx, dy = (along, perp) if di < 2 else (perp, along)
        ref = G.at[pl.ds(pl.multiple_of(block_row(dx, dy) + r0, QB), n)]
        s = SIGN[di]
        target = dev(s, 0, 0) if di < 2 else dev(0, s, 0)
        return pltpu.make_async_remote_copy(
            src_ref=ref, dst_ref=ref, send_sem=gs.at[di, j], recv_sem=gr.at[di, j],
            device_id=target, device_id_type=MESH)

    def g_send(di, j):
        g_copy(di, j, 0).start()

    def g_round(j):
        for di in range(4):
            s = SIGN[di]
            g_copy(di, j, 1).wait_recv()
            perp = (2, 3) if di < 2 else (0, 1)
            if j == 0:
                g_send(di, 2)
                for p in perp:
                    g_send(p, 3 if s > 0 else 4)
            elif j == 1:
                g_send(di, 5)
            elif j == 2:
                for p in perp:
                    g_send(p, 6 if s > 0 else 7)
            elif j == 3:
                g_send(di, 8)
            elif j == 4:
                g_send(di, 9)
            elif (j == 6 and s > 0) or (j == 7 and s < 0):
                g_send(di, 10)

    def a_ref(n, si, shift):
        s = 1 if si == 0 else -1
        d = (n // 2) if shift == 0 else (n // 2) + 1
        half = n % 2 if si == 0 else 1 - n % 2
        r = rem(z - s * d + NZ, NZ) * NC + k
        return AT.at[r, pl.ds(half * (DF // 2), DF // 2)]

    def a_copy(n, si, shift):
        ref = a_ref(n, si, shift)
        return pltpu.make_async_remote_copy(
            src_ref=ref, dst_ref=ref, send_sem=zs.at[si, n], recv_sem=zr.at[si, n],
            device_id=dev(0, 0, 1 if si == 0 else -1), device_id_type=MESH)

    SIB = (0, 1, -1, 2, -2, 3, -3, 4)

    def sib_copy(i, mine):
        r = rem(z - SIB[i] + NZ, NZ) * NC + (k if mine else 1 - k)
        return pltpu.make_async_remote_copy(
            src_ref=AT.at[r], dst_ref=AT.at[r], send_sem=sas.at[i], recv_sem=sar.at[i],
            device_id=dev(0, 0, 0, True), device_id_type=MESH)

    def a_round(n):
        for si in range(2):
            a_copy(n, si, 1).wait_recv()
            if n <= 4:
                a_copy(n + 2, si, 0).start()
            if n in (1, 3, 5):
                sib_copy(n + si, True).start()
        if n == 6:
            sib_copy(7, True).start()

    def pick(i, values):
        v = jnp.int32(values[-1])
        for q, e in enumerate(values[:-1]):
            v = jnp.where(i == q, e, v)
        return v

    def ig_blocks(blocks):
        rows = [pl.ds(pl.multiple_of(block_row(dxi, dyi), TB), TB) for dxi, dyi in blocks]

        for h in range(2):
            for n0 in range(0, DH, 256):
                lhs = jnp.concatenate([G[r, :] for r in rows], axis=0)
                d = jnp.dot(lhs, WT[:, h * DH + n0:h * DH + n0 + 256], preferred_element_type=F32)
                for i, (dxi, dyi) in enumerate(blocks):
                    PT[dxi * NY + dyi, h, :, n0:n0 + 256] = d[i * TB:(i + 1) * TB]
            for dxi, dyi in blocks:
                @pl.when(rem(dyi + y + k, 2) == 1)
                def _():
                    p_copy(dxi, dyi, h).start()

    def p_copy(dxi, dyi, h):
        idx, slot = dxi * NY + dyi, dxi * 2 + dyi // 2
        return pltpu.make_async_remote_copy(
            src_ref=PT.at[idx, h], dst_ref=PR.at[slot, h], send_sem=pss.at[idx, h], recv_sem=psr.at[slot, h],
            device_id=dev(0, 0, 0, True), device_id_type=MESH)

    parity = rem(y + k, 2)

    def unit(u):
        m, h = u // 2, rem(u, 2)
        t = jnp.where(parity == 0, rem(m, 4), m // 2)
        dxi = jnp.where(t == 1, 3, jnp.where(t == 2, 1, jnp.where(t == 3, 2, 0)))
        dyi = jnp.where(parity == 0, 2 * (m // 4), 1 + 2 * rem(m, 2))
        bx, by = rem(x + dxi, NX), rem(y + dyi, NY)
        owner = 2 * bx + by // 2
        delta = rem(z - owner + NZ, NZ)
        eps = jnp.where(h == 0, delta, rem(NZ - delta, NZ))
        return dxi, dyi, h, eps

    def c_copy(u, h, eps):
        slot = jnp.where(eps == 1, 1, 0)
        step = jnp.where((eps >= 4) == (h == 0), 1, NZ - 1)
        return pltpu.make_async_remote_copy(
            src_ref=CS.at[u], dst_ref=CR.at[u, slot], send_sem=css.at[u], recv_sem=crs.at[u, slot],
            device_id=(rem(z + step, NZ) * NC + k, col), device_id_type=MESH)

    def c_wait(u, slot):
        pltpu.make_async_remote_copy(
            src_ref=CS.at[u], dst_ref=CR.at[u, slot], send_sem=css.at[u], recv_sem=crs.at[u, slot],
            device_id=(row, col), device_id_type=MESH).wait_recv()

    def decode(u, slot, i, c, inv):
        code = CR[u, slot, pl.ds(pl.multiple_of(c * TB + i * 16, 16), 16), :].astype(F32)
        mag = (jnp.log(jnp.abs(code)) + REACH) * inv
        return jnp.where(code < 0.0, -mag, mag)

    def reduce_unit(u, p):
        dxi, dyi, h, eps = unit(u)
        idx, slot_p = dxi * NY + dyi, dxi * 2 + dyi // 2

        def collect(n):
            p_copy(dxi, dyi, h).wait_recv()
            for slot in range(n):
                c_wait(u, slot)
            return [CR[u, slot, KC:KC + SCR, :].astype(F32) * (1.0 / (2 * REACH)) for slot in range(n)]

        def total(i, c, invs):
            rr = pl.ds(pl.multiple_of(i * 16, 16), 16)
            cc = slice(c * 128, (c + 1) * 128)
            v = PT[idx, h, rr, cc] + PR[slot_p, h, rr, cc]
            for slot, inv in enumerate(invs):
                v = v + decode(u, slot, i, c, inv)
            return v

        def relay(n):
            invs = collect(n)

            def body(i, top):
                rr = pl.ds(pl.multiple_of(i * 16, 16), 16)
                for c in range(DH // 128):
                    v = total(i, c, invs)
                    PT[idx, h, rr, c * 128:(c + 1) * 128] = v
                    top = jnp.maximum(top, jnp.abs(v))
                return top

            top = lax.fori_loop(0, TB // 16, body, jnp.zeros((16, 128), F32))
            scale = jnp.maximum(top * 1.01, 1e-30).astype(BF16)
            CS[u, KC:KC + SCR, :] = scale
            mul = (2 * REACH) / scale.astype(F32)

            @pl.loop(0, TB // 16)
            def _(i):
                rr = pl.ds(pl.multiple_of(i * 16, 16), 16)
                for c in range(DH // 128):
                    v = PT[idx, h, rr, c * 128:(c + 1) * 128]
                    code = jnp.exp(jnp.abs(v) * mul - REACH)
                    code = jnp.where(v < 0.0, -code, code)
                    CS[u, pl.ds(pl.multiple_of(c * TB + i * 16, 16), 16), :] = code.astype(BF16)

            c_copy(u, h, eps).start()

        def finish(n):
            invs = collect(n)
            for half in range(2):
                @pl.when(h == half)
                def _():
                    @pl.loop(0, TB // 16)
                    def _(i):
                        rr = pl.ds(pl.multiple_of(i * 16, 16), 16)
                        for c in range(DH // 128):
                            c0 = half * DH + c * 128
                            ig_out[rr, c0:c0 + 128] = total(i, c, invs).astype(BF16)

        if p is None:
            pl.when(eps == 0)(lambda: finish(2))
        elif isinstance(p, int):
            pl.when((eps == 4) | (eps == 3))(lambda: relay(0))
        else:
            pl.when((eps == 4 + p) | ((eps == 3 - p) & (eps > 0)))(lambda: relay(1))

    def reduce_group(kind, items):
        @pl.loop(0, 2 * len(items))
        def _(i):
            j, h = i // 2, rem(i, 2)
            if kind == "middle":
                reduce_unit(2 * pick(j, [m for m, _ in items]) + h, pick(j, [p for _, p in items]))
            else:
                reduce_unit(2 * pick(j, items) + h, 0 if kind == "first" else None)

    def wg_step(b0, n0, n1, first, last):
        rows = pl.ds(pl.multiple_of(b0 * TB, TB), NY * TB)
        lhs = jnp.concatenate([AT[b0 + i] for i in range(NY)], axis=1)
        for n in range(n0, n1, 256):
            nn = slice(n, min(n + 256, n1))
            v = jnp.dot(lhs, G[rows, nn], preferred_element_type=F32)
            if last:
                wg_out[:, nn] = (ACC[:, nn] + v).astype(BF16)
            elif first:
                ACC[:, nn] = v
            else:
                ACC[:, nn] = ACC[:, nn] + v

    def wt_chunk(j):
        WT[j * 128:(j + 1) * 128, :] = W[:, j * 128:(j + 1) * 128].T

    load_a.wait()
    for j in range(DF // 128):
        AT[row, j * 128:(j + 1) * 128, :] = ABUF[:, j * 128:(j + 1) * 128].T
    load_g.wait()
    pl.semaphore_wait(barrier, len(partners))
    for j in range(2):
        for di in range(4):
            g_send(di, j)
        for si in range(2):
            a_copy(j, si, 0).start()
    sib_copy(0, True).start()
    load_w.wait()
    groups = {name: rem(x + int(name), NX) * NY for name in "0123"}
    wt_next, wg_done = 0, [0, 0]
    columns = ((0, 1024), (1024, FH))
    for what, *how in SCHEDULE:
        if what == "t":
            for j in range(wt_next, wt_next + how[0]):
                wt_chunk(j)
            wt_next += how[0]
        elif what == "g":
            g_round(how[0])
        elif what == "a":
            a_round(how[0])
        elif what == "i":
            ig_blocks(how[0])
        elif what == "s":
            for i in range(8):
                sib_copy(i, False).wait_recv()
        elif what == "w":
            part = how[1]
            wg_step(groups[how[0]], *columns[part], wg_done[part] == 0, wg_done[part] == 3)
            wg_done[part] += 1
        else:
            reduce_group(*how)

    for di in range(4):
        for j in range(11):
            g_copy(di, j, 0).wait_send()
    for si in range(2):
        for n in range(7):
            a_copy(n, si, 0).wait_send()
    for i in range(8):
        sib_copy(i, True).wait_send()

    @pl.loop(0, 16)
    def _(i):
        dxi, dyi = i // NY, rem(i, NY)

        @pl.when(rem(dyi + y + k, 2) == 1)
        def _():
            for h in range(2):
                p_copy(dxi, dyi, h).wait_send()

        _, _, h, eps = unit(i)

        @pl.when(eps != 0)
        def _():
            c_copy(i, h, eps).wait_send()


def hand_out(ig, wg, ig_out, wg_out, sems):
    n = sems.shape[0] - 1
    rows = DF // n
    copies = [pltpu.make_async_copy(wg.at[pl.ds(i * rows, rows)], wg_out.at[pl.ds(i * rows, rows)], sems.at[i])
              for i in range(n)]
    copies.append(pltpu.make_async_copy(ig, ig_out, sems.at[n]))
    for c in copies:
        c.start()
    for c in copies:
        c.wait()


def per_device(activations, out_grad, weight):
    dma = pltpu.SemaphoreType.DMA
    vmem = pltpu.VMEM
    nblk = NX * NY
    anywhere = pl.BlockSpec(memory_space=pl.ANY)
    sums = pl.pallas_call(
        kernel,
        name="up_backward",
        out_shape=(vmem((TB, DF), BF16), vmem((DF, FH), BF16)),
        in_specs=[anywhere] * 3,
        out_specs=(pl.BlockSpec(memory_space=vmem),) * 2,
        scratch_shapes=[
            vmem((nblk * TB, FH), BF16),
            vmem((NZ * NC, DF, TB), BF16),
            vmem((TB, DF), BF16),
            vmem((DF, FH), BF16),
            vmem((FH, DF), BF16),
            vmem((DF, FH), F32),
            vmem((nblk, 2, TB, DH), F32),
            vmem((nblk // 2, 2, TB, DH), F32),
            vmem((nblk, KC + SCR, 128), BF16),
            vmem((nblk, 2, KC + SCR, 128), BF16),
            dma((3,)),
            dma((4, 11)), dma((4, 11)),
            dma((2, 7)), dma((2, 7)),
            dma((8,)), dma((8,)),
            dma((nblk, 2)), dma((nblk // 2, 2)),
            dma((nblk,)), dma((nblk, 2)),
        ],
        cost_estimate=pl.CostEstimate(flops=4 * nblk * TB * DF * FH, bytes_accessed=8 * DF * FH, transcendentals=0),
        compiler_params=pltpu.CompilerParams(
            collective_id=0, has_side_effects=True, vmem_limit_bytes=52 << 20),
    )(activations, out_grad, weight)
    return pl.pallas_call(
        hand_out,
        name="hand_out",
        out_shape=(jax.ShapeDtypeStruct((TB, DF), BF16), jax.ShapeDtypeStruct((DF, FH), BF16)),
        in_specs=[pl.BlockSpec(memory_space=vmem)] * 2,
        out_specs=(anywhere, anywhere),
        scratch_shapes=[dma((17,))],
        compiler_params=pltpu.CompilerParams(vmem_limit_bytes=1 << 20),
    )(*sums)


def solution(mesh):
    placed = (P("row", "col"), P("col", "row"), P("col", "row"))
    return jax.shard_map(
        per_device,
        mesh=mesh,
        in_specs=placed,
        out_specs=(P("row", "col"), P("col", "row")),
        check_vma=False,
    )
```

```python
import functools

import jax
import jax.numpy as jnp
from jax import lax
from jax.experimental import pallas as pl
from jax.experimental.pallas import tpu as pltpu
from jax.sharding import PartitionSpec as P

NX, NY, NZ, NC = 4, 4, 8, 2
TB = 128
HB = TB // 2
QB = TB // 4
DF = 1024
FH = 1664
DH = DF // 2
KC = TB * DH // 128
SCR = 16
REACH = 85.0
MESH = pl.DeviceIdType.MESH
F32, BF16 = jnp.float32, jnp.bfloat16


SCHEDULE = (
    ('t', 7), ('t', 6), ('g', 0), ('a', 0), ('a', 1), ('a', 2), ('g', 1), ('i', ((0, 1), (0, 3))), ('g', 2), ('a', 3),
    ('i', ((1, 0), (3, 0))), ('r', 'first', (1,)), ('i', ((0, 0),)), ('g', 3), ('g', 4), ('r', 'first', (0,)),
    ('i', ((3, 3), (3, 1))), ('a', 4), ('i', ((1, 3), (1, 1))), ('r', 'middle', ((1, 1),)), ('g', 5),
    ('i', ((2, 0), (0, 2))), ('r', 'first', (3,)), ('g', 6), ('r', 'first', (2,)), ('g', 7), ('r', 'first', (4,)),
    ('a', 5), ('a', 6), ('g', 8), ('i', ((3, 2), (2, 3))), ('r', 'middle', ((3, 1), (1, 2))), ('r', 'first', (5,)),
    ('r', 'middle', ((2, 1),)), ('g', 9), ('i', ((1, 2), (2, 1))), ('g', 10), ('r', 'first', (6,)), ('i', ((2, 2),)),
    ('r', 'first', (7,)), ('r', 'middle', ((0, 1),)), ('s',), ('w', '1', 0), ('r', 'middle', ((4, 1), (5, 1))),
    ('w', '2', 1), ('r', 'middle', ((2, 2), (6, 1), (7, 1))), ('w', '0', 0), ('r', 'middle', ((3, 2), (0, 2))),
    ('w', '1', 1), ('r', 'middle', ((5, 2), (4, 2))), ('w', '2', 0), ('r', 'middle', ((6, 2), (7, 2))), ('w', '3', 1),
    ('w', '3', 0), ('r', 'middle', ((4, 3), (0, 3), (2, 3), (5, 3), (3, 3), (6, 3), (7, 3), (1, 3))), ('w', '0', 1),
    ('r', 'last', (2, 1, 5, 3, 4, 0, 6, 7)),
)

def rem(a, n):
    return lax.rem(a, n)


def kernel(
    act, og, w, ig_out, wg_out,
    G, AT, ABUF, W, WT, ACC, PT, PR, CS, CR,
    ld, gs, gr, zs, zr, sas, sar, pss, psr, css, crs,
):
    row, col = lax.axis_index("row"), lax.axis_index("col")
    z, k = row // NC, rem(row, NC)
    x, y = col // NY, rem(col, NY)

    def dev(dx, dy, dz, flip=False):
        kk = 1 - k if flip else k
        return (rem(z + dz + NZ, NZ) * NC + kk, rem(x + dx + NX, NX) * NY + rem(y + dy + NY, NY))

    def block_row(dx, dy):
        return (rem(x + dx + NX, NX) * NY + rem(y + dy + NY, NY)) * TB

    own = block_row(0, 0)
    load_g = pltpu.make_async_copy(og, G.at[pl.ds(pl.multiple_of(own, TB), TB)], ld.at[0])
    load_a = pltpu.make_async_copy(act, ABUF, ld.at[1])
    load_w = pltpu.make_async_copy(w, W, ld.at[2])
    load_a.start()
    load_g.start()
    load_w.start()

    partners = [dev(1, 0, 0), dev(-1, 0, 0), dev(0, 1, 0), dev(0, -1, 0), dev(0, 0, 1), dev(0, 0, -1),
                dev(0, 0, 0, True)]
    barrier = pltpu.get_barrier_semaphore()
    for d in partners:
        pl.semaphore_signal(barrier, inc=1, device_id=d, device_id_type=MESH)

    SIGN = (1, -1, 1, -1)

    def g_piece(di, j):
        s = SIGN[di]
        first, second = (0, HB) if di < 2 else (HB, 0)
        sub = 0 if s > 0 else QB
        along, perp, r0, n = (
            (0, 0, first, HB), (0, 0, second, HB), (-s, 0, first + sub, QB),
            (0, -1, second, HB), (0, 1, second, HB), (-s, 0, second + sub, QB),
            (0, 2, second, QB), (0, 2, second + QB, QB),
            (-s, -1, second + sub, QB), (-s, 1, second + sub, QB), (-s, 2, second + sub, QB),
        )[j]
        return along, perp, r0, n

    def g_copy(di, j, shift):
        along, perp, r0, n = g_piece(di, j)
        along = along - shift * SIGN[di]
        dx, dy = (along, perp) if di < 2 else (perp, along)
        ref = G.at[pl.ds(pl.multiple_of(block_row(dx, dy) + r0, QB), n)]
        s = SIGN[di]
        target = dev(s, 0, 0) if di < 2 else dev(0, s, 0)
        return pltpu.make_async_remote_copy(
            src_ref=ref, dst_ref=ref, send_sem=gs.at[di, j], recv_sem=gr.at[di, j],
            device_id=target, device_id_type=MESH)

    def g_send(di, j):
        g_copy(di, j, 0).start()

    def g_round(j):
        for di in range(4):
            s = SIGN[di]
            g_copy(di, j, 1).wait_recv()
            perp = (2, 3) if di < 2 else (0, 1)
            if j == 0:
                g_send(di, 2)
                for p in perp:
                    g_send(p, 3 if s > 0 else 4)
            elif j == 1:
                g_send(di, 5)
            elif j == 2:
                for p in perp:
                    g_send(p, 6 if s > 0 else 7)
            elif j == 3:
                g_send(di, 8)
            elif j == 4:
                g_send(di, 9)
            elif (j == 6 and s > 0) or (j == 7 and s < 0):
                g_send(di, 10)

    def a_ref(n, si, shift):
        s = 1 if si == 0 else -1
        d = (n // 2) if shift == 0 else (n // 2) + 1
        half = n % 2 if si == 0 else 1 - n % 2
        r = rem(z - s * d + NZ, NZ) * NC + k
        return AT.at[r, pl.ds(half * (DF // 2), DF // 2)]

    def a_copy(n, si, shift):
        ref = a_ref(n, si, shift)
        return pltpu.make_async_remote_copy(
            src_ref=ref, dst_ref=ref, send_sem=zs.at[si, n], recv_sem=zr.at[si, n],
            device_id=dev(0, 0, 1 if si == 0 else -1), device_id_type=MESH)

    SIB = (0, 1, -1, 2, -2, 3, -3, 4)

    def sib_copy(i, mine):
        r = rem(z - SIB[i] + NZ, NZ) * NC + (k if mine else 1 - k)
        return pltpu.make_async_remote_copy(
            src_ref=AT.at[r], dst_ref=AT.at[r], send_sem=sas.at[i], recv_sem=sar.at[i],
            device_id=dev(0, 0, 0, True), device_id_type=MESH)

    def a_round(n):
        for si in range(2):
            a_copy(n, si, 1).wait_recv()
            if n <= 4:
                a_copy(n + 2, si, 0).start()
            if n in (1, 3, 5):
                sib_copy(n + si, True).start()
        if n == 6:
            sib_copy(7, True).start()

    def pick(i, values):
        v = jnp.int32(values[-1])
        for q, e in enumerate(values[:-1]):
            v = jnp.where(i == q, e, v)
        return v

    def ig_blocks(blocks):
        rows = [pl.ds(pl.multiple_of(block_row(dxi, dyi), TB), TB) for dxi, dyi in blocks]

        for h in range(2):
            for n0 in range(0, DH, 256):
                lhs = jnp.concatenate([G[r, :] for r in rows], axis=0)
                d = jnp.dot(lhs, WT[:, h * DH + n0:h * DH + n0 + 256], preferred_element_type=F32)
                for i, (dxi, dyi) in enumerate(blocks):
                    PT[dxi * NY + dyi, h, :, n0:n0 + 256] = d[i * TB:(i + 1) * TB]
            for dxi, dyi in blocks:
                @pl.when(rem(dyi + y + k, 2) == 1)
                def _():
                    p_copy(dxi, dyi, h).start()

    def p_copy(dxi, dyi, h):
        idx, slot = dxi * NY + dyi, dxi * 2 + dyi // 2
        return pltpu.make_async_remote_copy(
            src_ref=PT.at[idx, h], dst_ref=PR.at[slot, h], send_sem=pss.at[idx, h], recv_sem=psr.at[slot, h],
            device_id=dev(0, 0, 0, True), device_id_type=MESH)

    parity = rem(y + k, 2)

    def unit(u):
        m, h = u // 2, rem(u, 2)
        t = jnp.where(parity == 0, rem(m, 4), m // 2)
        dxi = jnp.where(t == 1, 3, jnp.where(t == 2, 1, jnp.where(t == 3, 2, 0)))
        dyi = jnp.where(parity == 0, 2 * (m // 4), 1 + 2 * rem(m, 2))
        bx, by = rem(x + dxi, NX), rem(y + dyi, NY)
        owner = 2 * bx + by // 2
        delta = rem(z - owner + NZ, NZ)
        eps = jnp.where(h == 0, delta, rem(NZ - delta, NZ))
        return dxi, dyi, h, eps

    def c_copy(u, h, eps):
        slot = jnp.where(eps == 1, 1, 0)
        step = jnp.where((eps >= 4) == (h == 0), 1, NZ - 1)
        return pltpu.make_async_remote_copy(
            src_ref=CS.at[u], dst_ref=CR.at[u, slot], send_sem=css.at[u], recv_sem=crs.at[u, slot],
            device_id=(rem(z + step, NZ) * NC + k, col), device_id_type=MESH)

    def c_wait(u, slot):
        pltpu.make_async_remote_copy(
            src_ref=CS.at[u], dst_ref=CR.at[u, slot], send_sem=css.at[u], recv_sem=crs.at[u, slot],
            device_id=(row, col), device_id_type=MESH).wait_recv()

    def decode(u, slot, i, c, inv):
        code = CR[u, slot, pl.ds(pl.multiple_of(c * TB + i * 16, 16), 16), :].astype(F32)
        mag = (jnp.log(jnp.abs(code)) + REACH) * inv
        return jnp.where(code < 0.0, -mag, mag)

    def reduce_unit(u, p):
        dxi, dyi, h, eps = unit(u)
        idx, slot_p = dxi * NY + dyi, dxi * 2 + dyi // 2

        def collect(n):
            p_copy(dxi, dyi, h).wait_recv()
            for slot in range(n):
                c_wait(u, slot)
            return [CR[u, slot, KC:KC + SCR, :].astype(F32) * (1.0 / (2 * REACH)) for slot in range(n)]

        def total(i, c, invs):
            rr = pl.ds(pl.multiple_of(i * 16, 16), 16)
            cc = slice(c * 128, (c + 1) * 128)
            v = PT[idx, h, rr, cc] + PR[slot_p, h, rr, cc]
            for slot, inv in enumerate(invs):
                v = v + decode(u, slot, i, c, inv)
            return v

        def relay(n):
            invs = collect(n)

            def body(i, top):
                rr = pl.ds(pl.multiple_of(i * 16, 16), 16)
                for c in range(DH // 128):
                    v = total(i, c, invs)
                    PT[idx, h, rr, c * 128:(c + 1) * 128] = v
                    top = jnp.maximum(top, jnp.abs(v))
                return top

            top = lax.fori_loop(0, TB // 16, body, jnp.zeros((16, 128), F32), unroll=TB // 16)
            scale = jnp.maximum(top * 1.01, 1e-30).astype(BF16)
            CS[u, KC:KC + SCR, :] = scale
            mul = (2 * REACH) / scale.astype(F32)

            @pl.loop(0, TB // 16, unroll=TB // 16)
            def _(i):
                rr = pl.ds(pl.multiple_of(i * 16, 16), 16)
                for c in range(DH // 128):
                    v = PT[idx, h, rr, c * 128:(c + 1) * 128]
                    code = jnp.exp(jnp.abs(v) * mul - REACH)
                    code = jnp.where(v < 0.0, -code, code)
                    CS[u, pl.ds(pl.multiple_of(c * TB + i * 16, 16), 16), :] = code.astype(BF16)

            c_copy(u, h, eps).start()

        def finish(n):
            invs = collect(n)
            for half in range(2):
                @pl.when(h == half)
                def _():
                    @pl.loop(0, TB // 16, unroll=TB // 16)
                    def _(i):
                        rr = pl.ds(pl.multiple_of(i * 16, 16), 16)
                        for c in range(DH // 128):
                            c0 = half * DH + c * 128
                            ig_out[rr, c0:c0 + 128] = total(i, c, invs).astype(BF16)

        if p is None:
            pl.when(eps == 0)(lambda: finish(2))
        elif isinstance(p, int):
            pl.when((eps == 4) | (eps == 3))(lambda: relay(0))
        else:
            pl.when((eps == 4 + p) | ((eps == 3 - p) & (eps > 0)))(lambda: relay(1))

    def reduce_group(kind, items):
        @pl.loop(0, 2 * len(items))
        def _(i):
            j, h = i // 2, rem(i, 2)
            if kind == "middle":
                reduce_unit(2 * pick(j, [m for m, _ in items]) + h, pick(j, [p for _, p in items]))
            else:
                reduce_unit(2 * pick(j, items) + h, 0 if kind == "first" else None)

    def wg_step(b0, n0, n1, first, last):
        rows = pl.ds(pl.multiple_of(b0 * TB, TB), NY * TB)
        lhs = jnp.concatenate([AT[b0 + i] for i in range(NY)], axis=1)
        for n in range(n0, n1, 256):
            nn = slice(n, min(n + 256, n1))
            v = jnp.dot(lhs, G[rows, nn], preferred_element_type=F32)
            if last:
                wg_out[:, nn] = (ACC[:, nn] + v).astype(BF16)
            elif first:
                ACC[:, nn] = v
            else:
                ACC[:, nn] = ACC[:, nn] + v

    def wt_chunk(j):
        WT[j * 128:(j + 1) * 128, :] = W[:, j * 128:(j + 1) * 128].T

    load_a.wait()
    for j in range(DF // 128):
        AT[row, j * 128:(j + 1) * 128, :] = ABUF[:, j * 128:(j + 1) * 128].T
    load_g.wait()
    pl.semaphore_wait(barrier, len(partners))
    for j in range(2):
        for di in range(4):
            g_send(di, j)
        for si in range(2):
            a_copy(j, si, 0).start()
    sib_copy(0, True).start()
    load_w.wait()
    groups = {name: rem(x + int(name), NX) * NY for name in "0123"}
    wt_next, wg_done = 0, [0, 0]
    columns = ((0, 1024), (1024, FH))
    for what, *how in SCHEDULE:
        if what == "t":
            for j in range(wt_next, wt_next + how[0]):
                wt_chunk(j)
            wt_next += how[0]
        elif what == "g":
            g_round(how[0])
        elif what == "a":
            a_round(how[0])
        elif what == "i":
            ig_blocks(how[0])
        elif what == "s":
            for i in range(8):
                sib_copy(i, False).wait_recv()
        elif what == "w":
            part = how[1]
            wg_step(groups[how[0]], *columns[part], wg_done[part] == 0, wg_done[part] == 3)
            wg_done[part] += 1
        else:
            reduce_group(*how)

    for di in range(4):
        for j in range(11):
            g_copy(di, j, 0).wait_send()
    for si in range(2):
        for n in range(7):
            a_copy(n, si, 0).wait_send()
    for i in range(8):
        sib_copy(i, True).wait_send()

    @pl.loop(0, 16)
    def _(i):
        dxi, dyi = i // NY, rem(i, NY)

        @pl.when(rem(dyi + y + k, 2) == 1)
        def _():
            for h in range(2):
                p_copy(dxi, dyi, h).wait_send()

        _, _, h, eps = unit(i)

        @pl.when(eps != 0)
        def _():
            c_copy(i, h, eps).wait_send()


def hand_out(ig, wg, ig_out, wg_out, sems):
    n = sems.shape[0] - 1
    rows = DF // n
    copies = [pltpu.make_async_copy(wg.at[pl.ds(i * rows, rows)], wg_out.at[pl.ds(i * rows, rows)], sems.at[i])
              for i in range(n)]
    copies.append(pltpu.make_async_copy(ig, ig_out, sems.at[n]))
    for c in copies:
        c.start()
    for c in copies:
        c.wait()


def per_device(activations, out_grad, weight):
    dma = pltpu.SemaphoreType.DMA
    vmem = pltpu.VMEM
    nblk = NX * NY
    anywhere = pl.BlockSpec(memory_space=pl.ANY)
    sums = pl.pallas_call(
        kernel,
        name="up_backward",
        out_shape=(vmem((TB, DF), BF16), vmem((DF, FH), BF16)),
        in_specs=[anywhere] * 3,
        out_specs=(pl.BlockSpec(memory_space=vmem),) * 2,
        scratch_shapes=[
            vmem((nblk * TB, FH), BF16),
            vmem((NZ * NC, DF, TB), BF16),
            vmem((TB, DF), BF16),
            vmem((DF, FH), BF16),
            vmem((FH, DF), BF16),
            vmem((DF, FH), F32),
            vmem((nblk, 2, TB, DH), F32),
            vmem((nblk // 2, 2, TB, DH), F32),
            vmem((nblk, KC + SCR, 128), BF16),
            vmem((nblk, 2, KC + SCR, 128), BF16),
            dma((3,)),
            dma((4, 11)), dma((4, 11)),
            dma((2, 7)), dma((2, 7)),
            dma((8,)), dma((8,)),
            dma((nblk, 2)), dma((nblk // 2, 2)),
            dma((nblk,)), dma((nblk, 2)),
        ],
        cost_estimate=pl.CostEstimate(flops=4 * nblk * TB * DF * FH, bytes_accessed=8 * DF * FH, transcendentals=0),
        compiler_params=pltpu.CompilerParams(
            collective_id=0, has_side_effects=True, vmem_limit_bytes=52 << 20),
    )(activations, out_grad, weight)
    return pl.pallas_call(
        hand_out,
        name="hand_out",
        out_shape=(jax.ShapeDtypeStruct((TB, DF), BF16), jax.ShapeDtypeStruct((DF, FH), BF16)),
        in_specs=[pl.BlockSpec(memory_space=vmem)] * 2,
        out_specs=(anywhere, anywhere),
        scratch_shapes=[dma((17,))],
        compiler_params=pltpu.CompilerParams(vmem_limit_bytes=1 << 20),
    )(*sums)


def solution(mesh):
    placed = (P("row", "col"), P("col", "row"), P("col", "row"))
    return jax.shard_map(
        per_device,
        mesh=mesh,
        in_specs=placed,
        out_specs=(P("row", "col"), P("col", "row")),
        check_vma=False,
    )
```
